32 devices in a mesh: ctx: 8 (over z, x), fsdp: 4 (over y, core).
Axes of the slice: x: 2, y: 2, z: 4, core: 2. Of those that a mesh axis runs over, the one named last changes fastest.
Arguments:
- query: bfloat16 [2048, 2048], P('ctx', 'fsdp'), may hold values from -11 to 11
- key: bfloat16 [2048, 2048], P('ctx', 'fsdp'), may hold values from -11 to 11
- value: bfloat16 [2048, 2048], P('ctx', 'fsdp'), may hold values from -6 to 6
- doc_ids: int32 [2048], P('ctx'), may hold values from 0 to 5, never falling along the last dimension, each value on 1 to 512 neighbouring positions
- out_weight: bfloat16 [2048, 4096], P(('fsdp', 'ctx')), may hold values from -0.125 to 0.125
- grad_out: bfloat16 [2048, 4096], P('ctx', 'fsdp'), may hold values from -6 to 6
Outputs:
- grad_query: bfloat16 [2048, 2048], P('ctx', 'fsdp')
- grad_key: bfloat16 [2048, 2048], P('ctx', 'fsdp')
- grad_value: bfloat16 [2048, 2048], P('ctx', 'fsdp')
- grad_out_weight: float32 [2048, 4096], P(('fsdp', 'ctx'))
The draws below stay inside these ranges and needn't reach their ends.
Inputs may be any that keep to these rules, and one draw needn't show every extreme that they name: `doc_ids`: document ids never fall along the sequence; every document has 1 to 512 tokens and one has exactly 512.
All inputs are finite; a program needn't handle non-finite values.
Results may differ from the reference program's by a relative error of at most 0.034.
Values may be sent and summed in bfloat16 or wider, within the bound.
A program may use at most 128 MiB of HBM per device.

```python
import math
import jax
import jax.numpy as jnp
import numpy as np
from jax import lax

D = 4096
HEADS = 16
DH = 128
DOC_MOST = 512
DOCS = 6
SEQ = 2048


def draw_query(key, part):
    drawn = jnp.clip(jax.random.normal(jax.random.fold_in(key, 101), (SEQ, HEADS * DH), jnp.float32), -6.0, 6.0)
    return drawn.astype(jnp.bfloat16)


def draw_key(key, part):
    drawn = jnp.clip(jax.random.normal(jax.random.fold_in(key, 202), (SEQ, HEADS * DH), jnp.float32), -6.0, 6.0)
    return drawn.astype(jnp.bfloat16)


def shard_levels(rng, shape, shards, smallest, largest):
    level = 1.0
    for axis_at, blocks in shards:
        draws = jax.random.uniform(jax.random.fold_in(jax.random.fold_in(rng, 6), axis_at), (blocks,), jnp.float32, smallest / len(shards), largest / len(shards))
        level = level * jnp.repeat(jnp.exp(draws), shape[axis_at] // blocks).reshape((-1,) + (1,) * (len(shape) - 1 - axis_at))
    return level


def profile(number_of, total, reach, slope):
    weights = [(1 << 20) // math.isqrt(grade ** slope) + 1 for grade in range(2, number_of + 1)]
    rest, given = total - reach - (number_of - 1), [1] * (number_of - 1)
    while rest > 0:
        movable = [i for i in range(number_of - 1) if given[i] < reach]
        whole, budget = sum([weights[i] for i in movable]), rest
        for i in movable:
            more = min(reach - given[i], max(1, budget * weights[i] // whole), rest)
            given[i] = given[i] + more
            rest = rest - more
    return np.array([reach] + given)


def ragged_sizes(own_key, count, total, limit, skew):
    if count == 2:
        one = jax.random.randint(own_key, (), max(1, total - limit), min(limit, total - 1) + 1)
        return jnp.stack([one, total - one])
    lengths = jnp.asarray(profile(count, total, limit, skew), jnp.int32)
    couples = (count - 1) // 2
    source_of, taker = lengths[1:1 + 2 * couples:2], lengths[2:2 + 2 * couples:2]
    slack = jnp.minimum(source_of - 1, limit - taker)
    passed = jax.random.randint(jax.random.fold_in(own_key, 1), (couples,), 0, 1 << 20) % (slack + 1)
    lengths = lengths.at[1:1 + 2 * couples:2].set(source_of - passed).at[2:2 + 2 * couples:2].set(taker + passed)
    return lengths[jax.random.permutation(jax.random.fold_in(own_key, 2), count)]


def normal_values(key, shape, spread, limit, split=(), kind=jnp.bfloat16):
    values = jax.random.normal(key, shape, jnp.float32) * spread
    if len(split) > 0:
        values = shard_levels(key, shape, split, -0.22, 0.18) * values
    return jnp.clip(values, min=-limit, max=limit).astype(kind)


def setup_inputs(seed: int = 0) -> dict:
    key_list = jax.random.split(jax.random.key(seed), 7)
    return {
        "query": draw_query(jax.random.fold_in(key_list[6], 71), 0),
        "key": draw_key(jax.random.fold_in(key_list[6], 71), 0),
        "value": normal_values(key_list[2], (SEQ, HEADS * DH), 1.0, 6.0, ((0, 8), (1, 4))),
        "doc_ids": jnp.searchsorted(jnp.cumsum(ragged_sizes(key_list[3], DOCS, SEQ, DOC_MOST, 2)), jnp.arange(SEQ), side="right").astype(jnp.int32),
        "out_weight": normal_values(key_list[4], (HEADS * DH, D), (HEADS * DH) ** -0.5, 0.125, ((0, 32),)),
        "grad_out": normal_values(key_list[5], (SEQ, D), 1.0, 6.0, ((0, 8), (1, 4))),
    }


PRECISE = lax.Precision.HIGHEST
NEGATIVE = -1e+30

def head_major(array):
    return array.reshape(SEQ, HEADS, DH).transpose(1, 0, 2)

def reference(query, key, value, doc_ids, out_weight, grad_out):
    score_scale = 1.0 / math.sqrt(DH)
    block_rows = min(512, SEQ)
    block_count = SEQ // block_rows
    window_rows = DOC_MOST + block_rows
    token_docs = doc_ids.astype(jnp.int32)
    token_pos = jnp.arange(SEQ, dtype=jnp.int32)
    pad_docs = jnp.concatenate([jnp.full((DOC_MOST,), -1, jnp.int32), token_docs])
    pad_pos = jnp.arange(-DOC_MOST, SEQ, dtype=jnp.int32)

    def padded(array):
        return jnp.concatenate([jnp.zeros((HEADS, DOC_MOST, DH), array.dtype), array], axis=1)
    query_heads = head_major(query)
    key_pad = padded(head_major(key))
    value_pad = padded(head_major(value))

    def window(block_index, head_query, head_key):
        first_row = (block_index * block_rows).astype(jnp.int32)
        query_block = lax.dynamic_slice_in_dim(head_query, first_row, block_rows, 0)
        key_window = lax.dynamic_slice_in_dim(head_key, first_row, window_rows, 0)
        query_docs = lax.dynamic_slice_in_dim(token_docs, first_row, block_rows, 0)
        key_docs = lax.dynamic_slice_in_dim(pad_docs, first_row, window_rows, 0)
        query_pos = lax.dynamic_slice_in_dim(token_pos, first_row, block_rows, 0)
        key_pos = lax.dynamic_slice_in_dim(pad_pos, first_row, window_rows, 0)
        pair_mask = (query_docs[:, None] == key_docs[None, :]) & (key_pos[None, :] <= query_pos[:, None])
        scores = jnp.einsum('td,sd->ts', query_block.astype(jnp.float32), key_window.astype(jnp.float32), precision=PRECISE) * score_scale
        return (first_row, query_block, key_window, pair_mask, scores)

    def forward_head(head_index):
        head_query = query_heads[head_index]
        head_key = key_pad[head_index]
        head_value = value_pad[head_index]

        def one_block(block_index):
            first_row, query_block, key_window, pair_mask, scores = window(block_index, head_query, head_key)
            masked = jnp.where(pair_mask, scores, NEGATIVE)
            row_max = lax.optimization_barrier(jnp.max(masked, axis=-1))
            shifted = jnp.where(pair_mask, jnp.exp(masked - row_max[:, None]), 0.0)
            row_sum = lax.optimization_barrier(jnp.sum(shifted, axis=-1))
            log_total = row_max + jnp.log(row_sum)
            rounded = lax.optimization_barrier(shifted.astype(jnp.bfloat16)).astype(jnp.float32)
            value_window = lax.dynamic_slice_in_dim(head_value, first_row, window_rows, 0)
            output = jnp.einsum('ts,sd->td', rounded, value_window.astype(jnp.float32), precision=PRECISE) / row_sum[:, None]
            return (output, log_total)
        outputs, totals = lax.map(one_block, jnp.arange(block_count, dtype=jnp.int32))
        return (outputs.reshape(SEQ, DH), totals.reshape(SEQ))
    heads_out, heads_lse = lax.map(forward_head, jnp.arange(HEADS, dtype=jnp.int32))
    attn_heads = heads_out.astype(jnp.bfloat16)
    attention = attn_heads.transpose(1, 0, 2).reshape(SEQ, HEADS * DH)
    grad_attn = jnp.dot(grad_out, out_weight.T, preferred_element_type=jnp.float32).astype(jnp.bfloat16)
    grad_weight = jnp.dot(attention.T, grad_out, preferred_element_type=jnp.float32)
    grad_heads = head_major(grad_attn)
    delta_all = lax.optimization_barrier(jnp.sum(grad_heads.astype(jnp.float32) * attn_heads.astype(jnp.float32), axis=-1))

    def backward_head(head_index):
        head_query = query_heads[head_index]
        head_key = key_pad[head_index]
        head_value = value_pad[head_index]
        head_grad = grad_heads[head_index]
        head_lse = heads_lse[head_index]
        head_delta = delta_all[head_index]

        def one_block(carry, block_index):
            key_acc, value_acc = carry
            first_row, query_block, key_window, pair_mask, scores = window(block_index, head_query, head_key)
            value_window = lax.dynamic_slice_in_dim(head_value, first_row, window_rows, 0)
            grad_block = lax.dynamic_slice_in_dim(head_grad, first_row, block_rows, 0).astype(jnp.float32)
            lse_block = lax.dynamic_slice_in_dim(head_lse, first_row, block_rows, 0)
            delta_block = lax.dynamic_slice_in_dim(head_delta, first_row, block_rows, 0)
            weights = jnp.where(pair_mask, jnp.exp(scores - lse_block[:, None]), 0.0)
            rounded = weights.astype(jnp.bfloat16).astype(jnp.float32)
            value_part = jnp.einsum('ts,td->sd', rounded, grad_block, precision=PRECISE)
            grad_weights = jnp.einsum('td,sd->ts', grad_block, value_window.astype(jnp.float32), precision=PRECISE)
            grad_scores = (weights * (grad_weights - delta_block[:, None])).astype(jnp.bfloat16).astype(jnp.float32)
            query_part = jnp.einsum('ts,sd->td', grad_scores, key_window.astype(jnp.float32), precision=PRECISE) * score_scale
            key_part = jnp.einsum('ts,td->sd', grad_scores, query_block.astype(jnp.float32), precision=PRECISE) * score_scale
            key_old = lax.dynamic_slice_in_dim(key_acc, first_row, window_rows, 0)
            value_old = lax.dynamic_slice_in_dim(value_acc, first_row, window_rows, 0)
            key_acc = lax.dynamic_update_slice_in_dim(key_acc, key_old + key_part, first_row, 0)
            value_acc = lax.dynamic_update_slice_in_dim(value_acc, value_old + value_part, first_row, 0)
            return ((key_acc, value_acc), query_part)
        empty = jnp.zeros((SEQ + DOC_MOST, DH), jnp.float32)
        (key_acc, value_acc), query_parts = lax.scan(one_block, (empty, empty), jnp.arange(block_count, dtype=jnp.int32))
        return (query_parts.reshape(SEQ, DH), key_acc[DOC_MOST:], value_acc[DOC_MOST:])
    grad_q, grad_k, grad_v = lax.map(backward_head, jnp.arange(HEADS, dtype=jnp.int32))

    def token_major(array):
        return array.astype(jnp.bfloat16).transpose(1, 0, 2).reshape(SEQ, HEADS * DH)
    return (token_major(grad_q), token_major(grad_k), token_major(grad_v), grad_weight)
```

```python
import math

import jax
import jax.numpy as jnp
from jax import lax
from jax.experimental import pallas as pl
from jax.experimental.pallas import tpu as pltpu
from jax.sharding import PartitionSpec as P

DH = 128


NEGATIVE = -1e30


def shifted(array, axis, by):
    devices = lax.axis_size(axis)
    pairs = [(i, i + by) for i in range(devices) if 0 <= i + by < devices]
    return lax.ppermute(array, axis, pairs)


def as_sent(array):

    def short(part):
        return part.astype(jnp.bfloat16) if part.dtype == jnp.float32 else part

    return jax.tree.map(short, array)


def passed_along(block, axis, distance):
    devices = range(lax.axis_size(axis))
    route = [((i - distance) % len(devices), i) for i in devices]
    return lax.ppermute(block, axis, route)


def shards_general(query, key, value, doc_ids, out_weight, grad_out):
    tok_rows = query.shape[0]
    feature_width = query.shape[1]
    head_count = feature_width // DH
    cycle_size = lax.axis_size("ctx")
    cycle_reach = max(cycle_size // 8, 2)
    cycle_index = lax.axis_index("ctx")
    score_scale = 1.0 / math.sqrt(DH)
    local_pos = jnp.arange(tok_rows, dtype=jnp.int32)
    own_pos = cycle_index * tok_rows + local_pos
    own_docs = doc_ids + 1
    query_heads = query.reshape(tok_rows, head_count, DH)
    key_heads = key.reshape(tok_rows, head_count, DH)
    value_heads = value.reshape(tok_rows, head_count, DH)

    def scores_of(query_block, key_block):
        return (
            jnp.einsum("tnd,snd->nts", query_block, key_block, preferred_element_type=jnp.float32)
            * score_scale
        )

    state = (
        jnp.full((head_count, tok_rows), NEGATIVE, jnp.float32),
        jnp.zeros((head_count, tok_rows), jnp.float32),
        jnp.zeros((head_count, tok_rows, DH), jnp.float32),
    )
    key_block, value_block = (key_heads, value_heads)
    key_docs = own_docs
    stored_blocks = []
    for cycle_step in range(cycle_reach + 1):
        if cycle_step > 0:
            key_block, value_block = shifted((key_block, value_block), "ctx", 1)
            key_docs = shifted(key_docs, "ctx", 1)
        key_pos = own_pos - cycle_step * tok_rows
        pair_mask = (own_docs[:, None] == key_docs[None, :]) & (
            key_pos[None, :] <= own_pos[:, None]
        )
        forward_row_max, forward_row_sum, forward_output_sum = state
        forward_scores = jnp.where(pair_mask[None], scores_of(query_heads, key_block), NEGATIVE)
        new_max = jnp.maximum(forward_row_max, jnp.max(forward_scores, axis=-1))
        decay_factor = jnp.exp(forward_row_max - new_max)
        forward_weights = jnp.where(
            pair_mask[None], jnp.exp(forward_scores - new_max[..., None]), 0.0
        )
        new_sum = forward_row_sum * decay_factor + jnp.sum(forward_weights, axis=-1)
        weights_low = forward_weights.astype(jnp.bfloat16)
        new_output = forward_output_sum * decay_factor[..., None] + jnp.einsum(
            "nts,snd->ntd", weights_low, value_block, preferred_element_type=jnp.float32
        )
        state = (new_max, new_sum, new_output)
        stored_blocks.append((key_block, value_block, pair_mask))
    row_max, row_sum, output_sum = state
    log_total = row_max + jnp.log(row_sum)
    attn_heads = (output_sum / row_sum[..., None]).astype(jnp.bfloat16).transpose(1, 0, 2)
    attention = attn_heads.reshape(tok_rows, feature_width)
    grad_full = lax.all_gather(grad_out, "fsdp", axis=1, tiled=True)
    grad_attn = lax.dot_general(
        grad_full,
        lax.all_gather(out_weight, "ctx", axis=0, tiled=True),
        (((1,), (1,)), ((), ())),
        preferred_element_type=jnp.float32,
    ).astype(jnp.bfloat16)
    grad_weight = lax.psum_scatter(
        lax.dot_general(
            attention, grad_full, (((0,), (0,)), ((), ())), preferred_element_type=jnp.float32
        ),
        "ctx",
        scatter_dimension=0,
        tiled=True,
    )
    grad_heads = grad_attn.reshape(tok_rows, head_count, DH)
    delta_sum = jnp.einsum(
        "tnd,tnd->nt", grad_heads, attn_heads, preferred_element_type=jnp.float32
    )
    grad_query = jnp.zeros((tok_rows, head_count, DH), jnp.float32)
    carried = None
    for cycle_step in range(cycle_reach + 1):
        key_block, value_block, pair_mask = stored_blocks[cycle_step]
        if cycle_step > 0:
            carried = jax.tree.map(
                lambda part, own: part.astype(own.dtype),
                passed_along(as_sent(carried), "ctx", 1),
                carried,
            )
        scores = scores_of(query_heads, key_block)
        weights = jnp.where(pair_mask[None], jnp.exp(scores - log_total[..., None]), 0.0)
        rounded = weights.astype(jnp.bfloat16)
        value_part = jnp.einsum(
            "nts,tnd->snd", rounded, grad_heads, preferred_element_type=jnp.float32
        )
        grad_weights = jnp.einsum(
            "tnd,snd->nts", grad_heads, value_block, preferred_element_type=jnp.float32
        )
        grad_scores = (weights * (grad_weights - delta_sum[..., None])).astype(jnp.bfloat16)
        query_part = (
            jnp.einsum("nts,snd->tnd", grad_scores, key_block, preferred_element_type=jnp.float32)
            * score_scale
        )
        key_part = (
            jnp.einsum("nts,tnd->snd", grad_scores, query_heads, preferred_element_type=jnp.float32)
            * score_scale
        )
        query_part, key_part, value_part = (query_part, key_part, value_part)
        grad_query = grad_query + query_part
        if cycle_step == 0:
            carried = (key_part, value_part)
        else:
            carried = (carried[0] + key_part, carried[1] + value_part)
    grad_key, grad_value = jax.tree.map(
        lambda part, own: part.astype(own.dtype),
        passed_along(as_sent(carried), "ctx", -cycle_reach),
        carried,
    )
    return (
        grad_query.reshape(tok_rows, feature_width).astype(jnp.bfloat16),
        grad_key.reshape(tok_rows, feature_width).astype(jnp.bfloat16),
        grad_value.reshape(tok_rows, feature_width).astype(jnp.bfloat16),
        grad_weight,
    )


LINE = 4
F32 = jnp.float32
BF16 = jnp.bfloat16


def dot(a, b, dims):
    return lax.dot_general(a, b, (dims, ((), ())), preferred_element_type=F32)


def pair_kernel(
    q_ref, k_ref, v_ref, docrow_ref, doccol_ref, w_ref, g_ref,
    dq_ref, dk_ref, dv_ref, gw_ref,
    kwin, vwin, dwin, wall, gall, attn_pair, probs_all, part, up_out, down_out, up_in, down_in,
    pair_out, pair_in, ga_own, ga_out, ga_in, own_grads, grads_out, grads_in,
    local_sem, wx_send, wx_recv, w_send, w_recv, g_send, g_fwd, g_recv, kv_send, kv_recv,
    at_send, at_recv, up_send, up_recv, down_send, down_recv, px_send, px_recv,
    ga_send, ga_recv, gr_send, gr_recv,
):
    c = lax.axis_index("ctx")
    f = lax.axis_index("fsdp")
    z, x = c // 2, c % 2
    y, core = f // 2, f % 2
    rows = q_ref.shape[0]
    heads = q_ref.shape[1] // DH
    unit = w_ref.shape[0]
    width = g_ref.shape[1]
    scale = 1.0 / math.sqrt(DH)
    pending = []

    def remote(src, dst, ss, rs, dev):
        return pltpu.make_async_remote_copy(
            src_ref=src, dst_ref=dst, send_sem=ss, recv_sem=rs,
            device_id=dev, device_id_type=pl.DeviceIdType.MESH,
        )

    def send(src, dst, ss, rs, dev, cond=None):
        def start():
            remote(src, dst, ss, rs, dev).start()

        def finish():
            remote(src, dst, ss, rs, dev).wait_send()

        if cond is None:
            start()
        else:
            pl.when(cond)(start)
        pending.append((cond, finish))

    def arrived(dst, ss, rs):
        remote(dst, dst, ss, rs, (c, f)).wait_recv()

    pair = (c + 1 - 2 * x, f)
    up = (c + 2, f)
    down = (c - 2, f)
    has_up, has_down = z < LINE - 1, z > 0

    for step in range(2):
        there = c + 1 + step < 2 * LINE
        dev = (c + 1 + step, f)
        slot = pl.ds((1 - step) * rows, rows)
        send(docrow_ref, dwin.at[:, slot], kv_send.at[step, 0], kv_recv.at[step, 0], dev, there)
        send(k_ref, kwin.at[slot, :], kv_send.at[step, 1], kv_recv.at[step, 1], dev, there)
        send(v_ref, vwin.at[slot, :], kv_send.at[step, 2], kv_recv.at[step, 2], dev, there)

    mine = pl.ds(pl.multiple_of(x * unit, unit), unit)
    other = pl.ds(pl.multiple_of((1 - x) * unit, unit), unit)
    for j in range(2):
        cols = pl.ds(pl.multiple_of(2 * j * width + (1 - x) * width, width), width)
        send(
            w_ref.at[:, cols], wall.at[z, mine, pl.ds(j * width, width)],
            wx_send.at[j], wx_recv.at[j], pair,
        )
    local = []
    for j in range(2):
        cols = pl.ds(pl.multiple_of(2 * j * width + x * width, width), width)
        copy = pltpu.make_async_copy(
            w_ref.at[:, cols], wall.at[z, mine, pl.ds(j * width, width)], local_sem.at[j]
        )
        copy.start()
        local.append(copy)

    block = gall.at[
        pl.ds(pl.multiple_of(x * rows, rows), rows), pl.ds(pl.multiple_of(y * width, width), width)
    ]
    lead = core == x
    taker = 2 * z + core
    send(
        g_ref, block, g_send.at[0], g_recv.at[2 * x + y], (taker, 2 * (1 - y) + core)
    )
    send(
        g_ref, block, g_send.at[1], g_recv.at[2 * x + y], (taker, 2 * y + core), core != x
    )
    sibling = (c, f + 1 - 2 * core)

    @pl.when(lead)
    def _():
        pltpu.make_async_copy(g_ref, block, local_sem.at[2]).start()

    for copy in local:
        copy.wait()

    def spread(zb, rows_of, slot, rs, upward, downward):
        view = wall.at[zb, rows_of, :]
        if upward is not None:
            send(view, view, w_send.at[0, slot], rs, up, upward)
        if downward is not None:
            send(view, view, w_send.at[1, slot], rs, down, downward)

    spread(z, mine, 0, w_recv.at[z, x], has_up, has_down)
    for j in range(2):
        arrived(wall.at[z, other, pl.ds(j * width, width)], wx_send.at[j], wx_recv.at[j])
    spread(z, other, 1, w_recv.at[z, 1 - x], has_up, has_down)

    kwin[pl.ds(2 * rows, rows), :] = k_ref[...]
    vwin[pl.ds(2 * rows, rows), :] = v_ref[...]
    dwin[:, pl.ds(2 * rows, rows)] = docrow_ref[...]
    for step in range(2):
        slot = pl.ds((1 - step) * rows, rows)

        @pl.when(c < 1 + step)
        def _():
            kwin[slot, :] = jnp.zeros((rows, heads * DH), BF16)
            vwin[slot, :] = jnp.zeros((rows, heads * DH), BF16)
            dwin[:, slot] = jnp.full((8, rows), -1, jnp.int32)

        @pl.when(c + 1 + step >= 2 * LINE)
        def _():
            for h in range(heads):
                grads_in[h, step] = jnp.zeros((rows, 2 * DH), BF16)

    for xs in range(2):
        for ys in range(2):
            s = 2 * xs + ys
            view = gall.at[pl.ds(xs * rows, rows), pl.ds(ys * width, width)]
            own = (x == xs) & (y == ys)

            @pl.when(lead & own)
            def _():
                pltpu.make_async_copy(g_ref, view, local_sem.at[2]).wait()

            @pl.when(lead & jnp.logical_not(own))
            def _():
                arrived(view, g_fwd.at[s], g_recv.at[s])

            send(view, view, g_fwd.at[s], g_recv.at[s], sibling, lead)

    for step in range(2):
        slot = pl.ds((1 - step) * rows, rows)

        @pl.when(c >= 1 + step)
        def _():
            arrived(dwin.at[:, slot], kv_send.at[step, 0], kv_recv.at[step, 0])
            arrived(kwin.at[slot, :], kv_send.at[step, 1], kv_recv.at[step, 1])
            arrived(vwin.at[slot, :], kv_send.at[step, 2], kv_recv.at[step, 2])

    window = 3 * rows
    here = pl.ds(pl.multiple_of(x * rows, rows), rows)
    there = pl.ds(pl.multiple_of((1 - x) * rows, rows), rows)
    t_pos = lax.broadcasted_iota(jnp.int32, (rows, window), 0) + 2 * rows
    j_pos = lax.broadcasted_iota(jnp.int32, (rows, window), 1)
    mask = (doccol_ref[...] == dwin[0:1, :]) & (j_pos <= t_pos)
    for h in range(heads):
        hc = pl.ds(h * DH, DH)
        scores = dot(q_ref[:, hc], kwin[:, hc], ((1,), (1,))) * scale
        scores = jnp.where(mask, scores, NEGATIVE)
        top = jnp.max(scores, axis=1, keepdims=True)
        weights = jnp.where(mask, jnp.exp(scores - top), 0.0)
        inverse = 1.0 / jnp.sum(weights, axis=1, keepdims=True)
        out = dot(weights.astype(BF16), vwin[:, hc], ((1,), (0,))) * inverse
        probs_all[h] = weights * inverse
        attn_pair[here, hc] = out.astype(BF16)
    send(attn_pair.at[here, :], attn_pair.at[here, :], at_send, at_recv, pair)

    def w_round(r):
        for u in range(2):
            view_of = pl.ds(u * unit, unit)

            @pl.when(z - r >= 0)
            def _():
                arrived(wall.at[z - r, view_of, :], w_send.at[0, 2 * r + u], w_recv.at[z - r, u])

            if r < LINE - 1:
                spread(
                    z - r, view_of, 2 * r + u, w_recv.at[z - r, u], (z - r >= 0) & has_up, None
                )

            @pl.when(z + r < LINE)
            def _():
                arrived(wall.at[z + r, view_of, :], w_send.at[1, 2 * r + u], w_recv.at[z + r, u])

            if r < LINE - 1:
                send(
                    wall.at[z + r, view_of, :], wall.at[z + r, view_of, :],
                    w_send.at[1, 2 * r + u], w_recv.at[z + r, u], down, (z + r < LINE) & has_down,
                )

    w_round(1)

    for s in range(4):
        @pl.when(jnp.logical_not(lead))
        def _():
            arrived(
                gall.at[pl.ds((s // 2) * rows, rows), pl.ds((s % 2) * width, width)],
                g_fwd.at[s], g_recv.at[s],
            )

    arrived(attn_pair.at[there, :], at_send, at_recv)
    for b in range(LINE):
        part[b] = dot(attn_pair[:, pl.ds(b * DH, DH)], gall[...], ((0,), (0,)))

    def sum_step(s):
        b_up = LINE - 1 - s + z
        b_down = s - (LINE - 1) + z
        goes_up = (z <= s) & has_up
        goes_down = (LINE - 1 - z <= s) & has_down

        @pl.when(goes_up & jnp.logical_not(has_down))
        def _():
            up_out[s] = part[b_up].astype(BF16)

        @pl.when(goes_up & has_down)
        def _():
            arrived(up_in.at[b_up], up_send.at[s], up_recv.at[b_up])
            up_out[s] = (part[b_up] + up_in[b_up].astype(F32)).astype(BF16)

        send(up_out.at[s], up_in.at[b_up], up_send.at[s], up_recv.at[b_up], up, goes_up)

        @pl.when(goes_down & jnp.logical_not(has_up))
        def _():
            down_out[s] = part[b_down].astype(BF16)

        @pl.when(goes_down & has_up)
        def _():
            arrived(down_in.at[b_down], down_send.at[s], down_recv.at[b_down])
            down_out[s] = (part[b_down] + down_in[b_down].astype(F32)).astype(BF16)

        send(
            down_out.at[s], down_in.at[b_down], down_send.at[s], down_recv.at[b_down],
            down, goes_down,
        )

    sum_step(0)
    w_round(2)
    sum_step(1)
    w_round(3)

    for h in range(heads):
        ga = dot(gall[...], wall[h], ((1,), (1,)))
        ga_own[h] = ga
        ga_out[h] = ga_own[h, there, :].astype(BF16)
        send(ga_out.at[h], ga_in.at[h], ga_send.at[h], ga_recv.at[h], pair)

    sum_step(2)

    for h in range(heads):
        hc = pl.ds(h * DH, DH)
        arrived(ga_in.at[h], ga_send.at[h], ga_recv.at[h])
        ga = (ga_own[h, here, :] + ga_in[h].astype(F32)).astype(BF16)
        delta = jnp.sum(
            ga.astype(F32) * attn_pair[here, hc].astype(F32), axis=1, keepdims=True
        )
        probs = probs_all[h]
        grad_v = dot(probs.astype(BF16), ga, ((0,), (0,)))
        grad_p = dot(ga, vwin[:, hc], ((1,), (1,)))
        grad_s = (probs * (grad_p - delta)).astype(BF16)
        dq_ref[:, hc] = (dot(grad_s, kwin[:, hc], ((1,), (0,))) * scale).astype(BF16)
        grad_k = dot(grad_s, q_ref[:, hc], ((0,), (0,))) * scale
        for step in range(2):
            first = (1 - step) * rows
            grads_out[h, step, :, pl.ds(0, DH)] = grad_k[first:first + rows].astype(BF16)
            grads_out[h, step, :, pl.ds(DH, DH)] = grad_v[first:first + rows].astype(BF16)
            send(
                grads_out.at[h, step], grads_in.at[h, step], gr_send.at[h, step],
                gr_recv.at[h, step], (c - 1 - step, f), c >= 1 + step,
            )
        own_grads[h, :, pl.ds(0, DH)] = grad_k[2 * rows:]
        own_grads[h, :, pl.ds(DH, DH)] = grad_v[2 * rows:]

    @pl.when(has_down)
    def _():
        arrived(up_in.at[z], up_send.at[0], up_recv.at[z])
        part[z] = part[z] + up_in[z].astype(F32)

    @pl.when(has_up)
    def _():
        arrived(down_in.at[z], down_send.at[0], down_recv.at[z])
        part[z] = part[z] + down_in[z].astype(F32)

    pair_out[...] = part[z, other, :].astype(BF16)
    send(pair_out, pair_in, px_send, px_recv, pair)
    for xs in range(2):
        @pl.when(x == xs)
        def _():
            for j in range(2):
                gw_ref[:, pl.ds((2 * j + xs) * width, width)] = part[
                    z, pl.ds(xs * unit, unit), pl.ds(j * width, width)
                ]

    for h in range(heads):
        hc = pl.ds(h * DH, DH)
        for step in range(2):
            @pl.when(c + 1 + step < 2 * LINE)
            def _():
                arrived(grads_in.at[h, step], gr_send.at[h, step], gr_recv.at[h, step])
        total = own_grads[h] + grads_in[h, 0].astype(F32) + grads_in[h, 1].astype(F32)
        dk_ref[:, hc] = total[:, :DH].astype(BF16)
        dv_ref[:, hc] = total[:, DH:].astype(BF16)

    arrived(pair_in, px_send, px_recv)
    for xs in range(2):
        @pl.when(x == xs)
        def _():
            for j in range(2):
                gw_ref[:, pl.ds((2 * j + 1 - xs) * width, width)] = pair_in[
                    :, pl.ds(j * width, width)
                ].astype(F32)

    for cond, finish in pending:
        if cond is None:
            finish()
        else:
            pl.when(cond)(finish)


def shards_pairs(query, key, value, doc_ids, out_weight, grad_out):
    rows, cols = query.shape
    heads = cols // DH
    unit, feats = out_weight.shape
    width = grad_out.shape[1]
    half = 2 * width
    dma = pltpu.SemaphoreType.DMA
    vm = pl.BlockSpec(memory_space=pltpu.VMEM)
    doc_row = jnp.broadcast_to(doc_ids[None, :], (8, rows))
    doc_col = doc_ids[:, None]
    return pl.pallas_call(
        pair_kernel,
        out_shape=(
            jax.ShapeDtypeStruct((rows, cols), BF16),
            jax.ShapeDtypeStruct((rows, cols), BF16),
            jax.ShapeDtypeStruct((rows, cols), BF16),
            jax.ShapeDtypeStruct((unit, feats), F32),
        ),
        in_specs=[vm] * 7,
        out_specs=(vm,) * 4,
        scratch_shapes=[
            pltpu.VMEM((3 * rows, cols), BF16),
            pltpu.VMEM((3 * rows, cols), BF16),
            pltpu.VMEM((8, 3 * rows), jnp.int32),
            pltpu.VMEM((LINE, 2 * unit, half), BF16),
            pltpu.VMEM((2 * rows, half), BF16),
            pltpu.VMEM((2 * rows, cols), BF16),
            pltpu.VMEM((heads, rows, 3 * rows), F32),
            pltpu.VMEM((LINE, 2 * unit, half), F32),
            pltpu.VMEM((LINE - 1, 2 * unit, half), BF16),
            pltpu.VMEM((LINE - 1, 2 * unit, half), BF16),
            pltpu.VMEM((LINE, 2 * unit, half), BF16),
            pltpu.VMEM((LINE, 2 * unit, half), BF16),
            pltpu.VMEM((unit, half), BF16),
            pltpu.VMEM((unit, half), BF16),
            pltpu.VMEM((heads, 2 * rows, DH), F32),
            pltpu.VMEM((heads, rows, DH), BF16),
            pltpu.VMEM((heads, rows, DH), BF16),
            pltpu.VMEM((heads, rows, 2 * DH), F32),
            pltpu.VMEM((heads, 2, rows, 2 * DH), BF16),
            pltpu.VMEM((heads, 2, rows, 2 * DH), BF16),
            dma((3,)),
            dma((2,)), dma((2,)),
            dma((2, 2 * LINE)), dma((LINE, 2)),
            dma((2,)), dma((4,)), dma((4,)),
            dma((2, 3)), dma((2, 3)),
            dma, dma,
            dma((LINE,)), dma((LINE,)), dma((LINE,)), dma((LINE,)),
            dma, dma,
            dma((heads,)), dma((heads,)),
            dma((heads, 2)), dma((heads, 2)),
        ],
        compiler_params=pltpu.CompilerParams(
            has_side_effects=True, vmem_limit_bytes=56 * 1024 * 1024
        ),
    )(query, key, value, doc_row, doc_col, out_weight, grad_out)


def solution(mesh):
    return jax.shard_map(
        shards_pairs if mesh.shape["ctx"] == 8 and mesh.shape["fsdp"] == 4 else shards_general,
        mesh=mesh,
        in_specs=(
            P("ctx", "fsdp"),
            P("ctx", "fsdp"),
            P("ctx", "fsdp"),
            P("ctx"),
            P(("fsdp", "ctx"), None),
            P("ctx", "fsdp"),
        ),
        out_specs=(P("ctx", "fsdp"), P("ctx", "fsdp"), P("ctx", "fsdp"), P(("fsdp", "ctx"), None)),
        check_vma=False,
    )
```

```python
import math

import jax
import jax.numpy as jnp
from jax import lax
from jax.experimental import pallas as pl
from jax.experimental.pallas import tpu as pltpu
from jax.sharding import PartitionSpec as P

DH = 128


NEGATIVE = -1e30


def shifted(array, axis, by):
    devices = lax.axis_size(axis)
    pairs = [(i, i + by) for i in range(devices) if 0 <= i + by < devices]
    return lax.ppermute(array, axis, pairs)


def as_sent(array):

    def short(part):
        return part.astype(jnp.bfloat16) if part.dtype == jnp.float32 else part

    return jax.tree.map(short, array)


def passed_along(block, axis, distance):
    devices = range(lax.axis_size(axis))
    route = [((i - distance) % len(devices), i) for i in devices]
    return lax.ppermute(block, axis, route)


def shards_general(query, key, value, doc_ids, out_weight, grad_out):
    tok_rows = query.shape[0]
    feature_width = query.shape[1]
    head_count = feature_width // DH
    cycle_size = lax.axis_size("ctx")
    cycle_reach = max(cycle_size // 8, 2)
    cycle_index = lax.axis_index("ctx")
    score_scale = 1.0 / math.sqrt(DH)
    local_pos = jnp.arange(tok_rows, dtype=jnp.int32)
    own_pos = cycle_index * tok_rows + local_pos
    own_docs = doc_ids + 1
    query_heads = query.reshape(tok_rows, head_count, DH)
    key_heads = key.reshape(tok_rows, head_count, DH)
    value_heads = value.reshape(tok_rows, head_count, DH)

    def scores_of(query_block, key_block):
        return (
            jnp.einsum("tnd,snd->nts", query_block, key_block, preferred_element_type=jnp.float32)
            * score_scale
        )

    state = (
        jnp.full((head_count, tok_rows), NEGATIVE, jnp.float32),
        jnp.zeros((head_count, tok_rows), jnp.float32),
        jnp.zeros((head_count, tok_rows, DH), jnp.float32),
    )
    key_block, value_block = (key_heads, value_heads)
    key_docs = own_docs
    stored_blocks = []
    for cycle_step in range(cycle_reach + 1):
        if cycle_step > 0:
            key_block, value_block = shifted((key_block, value_block), "ctx", 1)
            key_docs = shifted(key_docs, "ctx", 1)
        key_pos = own_pos - cycle_step * tok_rows
        pair_mask = (own_docs[:, None] == key_docs[None, :]) & (
            key_pos[None, :] <= own_pos[:, None]
        )
        forward_row_max, forward_row_sum, forward_output_sum = state
        forward_scores = jnp.where(pair_mask[None], scores_of(query_heads, key_block), NEGATIVE)
        new_max = jnp.maximum(forward_row_max, jnp.max(forward_scores, axis=-1))
        decay_factor = jnp.exp(forward_row_max - new_max)
        forward_weights = jnp.where(
            pair_mask[None], jnp.exp(forward_scores - new_max[..., None]), 0.0
        )
        new_sum = forward_row_sum * decay_factor + jnp.sum(forward_weights, axis=-1)
        weights_low = forward_weights.astype(jnp.bfloat16)
        new_output = forward_output_sum * decay_factor[..., None] + jnp.einsum(
            "nts,snd->ntd", weights_low, value_block, preferred_element_type=jnp.float32
        )
        state = (new_max, new_sum, new_output)
        stored_blocks.append((key_block, value_block, pair_mask))
    row_max, row_sum, output_sum = state
    log_total = row_max + jnp.log(row_sum)
    attn_heads = (output_sum / row_sum[..., None]).astype(jnp.bfloat16).transpose(1, 0, 2)
    attention = attn_heads.reshape(tok_rows, feature_width)
    grad_full = lax.all_gather(grad_out, "fsdp", axis=1, tiled=True)
    grad_attn = lax.dot_general(
        grad_full,
        lax.all_gather(out_weight, "ctx", axis=0, tiled=True),
        (((1,), (1,)), ((), ())),
        preferred_element_type=jnp.float32,
    ).astype(jnp.bfloat16)
    grad_weight = lax.psum_scatter(
        lax.dot_general(
            attention, grad_full, (((0,), (0,)), ((), ())), preferred_element_type=jnp.float32
        ),
        "ctx",
        scatter_dimension=0,
        tiled=True,
    )
    grad_heads = grad_attn.reshape(tok_rows, head_count, DH)
    delta_sum = jnp.einsum(
        "tnd,tnd->nt", grad_heads, attn_heads, preferred_element_type=jnp.float32
    )
    grad_query = jnp.zeros((tok_rows, head_count, DH), jnp.float32)
    carried = None
    for cycle_step in range(cycle_reach + 1):
        key_block, value_block, pair_mask = stored_blocks[cycle_step]
        if cycle_step > 0:
            carried = jax.tree.map(
                lambda part, own: part.astype(own.dtype),
                passed_along(as_sent(carried), "ctx", 1),
                carried,
            )
        scores = scores_of(query_heads, key_block)
        weights = jnp.where(pair_mask[None], jnp.exp(scores - log_total[..., None]), 0.0)
        rounded = weights.astype(jnp.bfloat16)
        value_part = jnp.einsum(
            "nts,tnd->snd", rounded, grad_heads, preferred_element_type=jnp.float32
        )
        grad_weights = jnp.einsum(
            "tnd,snd->nts", grad_heads, value_block, preferred_element_type=jnp.float32
        )
        grad_scores = (weights * (grad_weights - delta_sum[..., None])).astype(jnp.bfloat16)
        query_part = (
            jnp.einsum("nts,snd->tnd", grad_scores, key_block, preferred_element_type=jnp.float32)
            * score_scale
        )
        key_part = (
            jnp.einsum("nts,tnd->snd", grad_scores, query_heads, preferred_element_type=jnp.float32)
            * score_scale
        )
        query_part, key_part, value_part = (query_part, key_part, value_part)
        grad_query = grad_query + query_part
        if cycle_step == 0:
            carried = (key_part, value_part)
        else:
            carried = (carried[0] + key_part, carried[1] + value_part)
    grad_key, grad_value = jax.tree.map(
        lambda part, own: part.astype(own.dtype),
        passed_along(as_sent(carried), "ctx", -cycle_reach),
        carried,
    )
    return (
        grad_query.reshape(tok_rows, feature_width).astype(jnp.bfloat16),
        grad_key.reshape(tok_rows, feature_width).astype(jnp.bfloat16),
        grad_value.reshape(tok_rows, feature_width).astype(jnp.bfloat16),
        grad_weight,
    )


LINE = 4
F32 = jnp.float32
BF16 = jnp.bfloat16


def dot(a, b, dims):
    return lax.dot_general(a, b, (dims, ((), ())), preferred_element_type=F32)


def pair_kernel(
    q_ref, k_ref, v_ref, doc_ref, w_ref, g_ref,
    dq_ref, dk_ref, dv_ref, gw_ref,
    docs, kwin, vwin, dwin, wall, gall, attn_pair, probs_all, part, up_out, down_out, up_in, down_in,
    pair_out, pair_in, ga_own, ga_out, ga_in, own_grads, grads_out, grads_in,
    fold_in, fold_out,
    local_sem, wx_send, wx_recv, w_send, w_recv, g_send, g_fwd, g_recv, kv_send, kv_recv,
    kp_send, kp_fwd, kp_recv,
    at_send, at_recv, up_send, up_recv, down_send, down_recv, px_send, px_recv,
    ga_send, ga_recv, gr_send, gr_recv, fold_send, fold_recv,
):
    c = lax.axis_index("ctx")
    f = lax.axis_index("fsdp")
    z, x = c // 2, c % 2
    y, core = f // 2, f % 2
    rows = q_ref.shape[0]
    heads = q_ref.shape[1] // DH
    unit = w_ref.shape[0]
    width = g_ref.shape[1]
    scale = 1.0 / math.sqrt(DH)
    pending = []

    def remote(src, dst, ss, rs, dev):
        return pltpu.make_async_remote_copy(
            src_ref=src, dst_ref=dst, send_sem=ss, recv_sem=rs,
            device_id=dev, device_id_type=pl.DeviceIdType.MESH,
        )

    def send(src, dst, ss, rs, dev, cond=None):
        def start():
            remote(src, dst, ss, rs, dev).start()

        def finish():
            remote(src, dst, ss, rs, dev).wait_send()

        if cond is None:
            start()
        else:
            pl.when(cond)(start)
        pending.append((cond, finish))

    def arrived(dst, ss, rs):
        remote(dst, dst, ss, rs, (c, f)).wait_recv()

    pair = (c + 1 - 2 * x, f)
    up = (c + 2, f)
    down = (c - 2, f)
    has_up, has_down = z < LINE - 1, z > 0

    barrier = pltpu.get_barrier_semaphore()

    def greet(dev):
        pl.semaphore_signal(barrier, inc=1, device_id=dev, device_id_type=pl.DeviceIdType.MESH)

    greet(pair)
    greet((c, f + 1 - 2 * core))
    greet((c, f + 2 - 4 * y))
    greet((c + 1 - 2 * x, f + 2 - 4 * y))
    pl.when(has_up)(lambda: greet(up))
    pl.when(has_down)(lambda: greet(down))
    pl.semaphore_wait(barrier, 4 + (z + LINE - 1) // LINE + (2 * LINE - 2 - z) // LINE)

    docs[...] = jnp.broadcast_to(doc_ref[...], (8, rows))
    halfc = heads * DH // 2
    backward_order = 1 - z // 2
    backward_order_up = 1 - (z + 1) // 2
    first, second, last = (pl.ds(i * rows, rows) for i in range(3))

    def half_cols(i, backward):
        return pl.ds(pl.multiple_of((i + (1 - 2 * i) * backward) * halfc, halfc), halfc)

    send(docs, dwin.at[:, first], kv_send.at[2, 0], kv_recv.at[2, 0], up, has_up)
    send(docs, dwin.at[:, second], kp_send.at[2, 0], kp_recv.at[2, 0], pair, x == 0)
    for i in range(2):
        hu, hp = half_cols(i, backward_order_up), half_cols(i, backward_order)
        for n, (own, win) in enumerate(((k_ref, kwin), (v_ref, vwin))):
            send(own.at[:, hu], win.at[first, hu], kv_send.at[i, n], kv_recv.at[i, n], up, has_up)
            send(own.at[:, hp], win.at[second, hp], kp_send.at[i, n], kp_recv.at[i, n], pair, x == 0)

    mine = pl.ds(pl.multiple_of(x * unit, unit), unit)
    other = pl.ds(pl.multiple_of((1 - x) * unit, unit), unit)
    for j in range(2):
        cols = pl.ds(pl.multiple_of(2 * j * width + (1 - x) * width, width), width)
        send(
            w_ref.at[:, cols], wall.at[z, mine, pl.ds(j * width, width)],
            wx_send.at[j], wx_recv.at[j], pair,
        )
    local = []
    for j in range(2):
        cols = pl.ds(pl.multiple_of(2 * j * width + x * width, width), width)
        copy = pltpu.make_async_copy(
            w_ref.at[:, cols], wall.at[z, mine, pl.ds(j * width, width)], local_sem.at[j]
        )
        copy.start()
        local.append(copy)

    block = gall.at[
        pl.ds(pl.multiple_of(x * rows, rows), rows), pl.ds(pl.multiple_of(y * width, width), width)
    ]
    lead = core == x
    taker = 2 * z + core
    send(
        g_ref, block, g_send.at[0], g_recv.at[2 * x + y], (taker, 2 * (1 - y) + core)
    )
    send(
        g_ref, block, g_send.at[1], g_recv.at[2 * x + y], (taker, 2 * y + core), core != x
    )
    sibling = (c, f + 1 - 2 * core)

    @pl.when(lead)
    def _():
        pltpu.make_async_copy(g_ref, block, local_sem.at[2]).start()

    for copy in local:
        copy.wait()

    def spread(zb, rows_of, slot, rs, upward, downward):
        view = wall.at[zb, rows_of, :]
        if upward is not None:
            send(view, view, w_send.at[0, slot], rs, up, upward)
        if downward is not None:
            send(view, view, w_send.at[1, slot], rs, down, downward)

    spread(z, mine, 0, w_recv.at[z, x], None, has_down)
    for j in range(2):
        arrived(wall.at[z, other, pl.ds(j * width, width)], wx_send.at[j], wx_recv.at[j])
    spread(z, other, 1, w_recv.at[z, 1 - x], None, has_down)

    kwin[last, :] = k_ref[...]
    vwin[last, :] = v_ref[...]
    dwin[:, last] = docs[...]

    def nothing(slot):
        kwin[slot, :] = jnp.zeros((rows, heads * DH), BF16)
        vwin[slot, :] = jnp.zeros((rows, heads * DH), BF16)
        dwin[:, slot] = jnp.full((8, rows), -1, jnp.int32)

    pl.when(z == 0)(lambda: nothing(first))
    pl.when((z == 0) & (x == 0))(lambda: nothing(second))

    relay = (x == 1) & has_down

    def relayed(part_of, ss, rs, fs, ps):
        src = part_of(first)

        @pl.when(has_down)
        def _():
            arrived(src, ss, rs)

        send(src, part_of(second), fs, ps, pair, relay)

    def take(part_of, ss, ps):
        @pl.when((x == 1) | has_down)
        def _():
            arrived(part_of(second), ss, ps)

    def win_part(win, cols):
        return lambda slot: win.at[slot, cols]

    def doc_part(slot):
        return dwin.at[:, slot]

    relayed(doc_part, kv_send.at[2, 0], kv_recv.at[2, 0], kp_fwd.at[2, 0], kp_recv.at[2, 0])
    for i in range(2):
        for n, win in enumerate((kwin, vwin)):
            relayed(
                win_part(win, half_cols(i, backward_order)),
                kv_send.at[i, n], kv_recv.at[i, n], kp_fwd.at[i, n], kp_recv.at[i, n],
            )
    spread(z, mine, 0, w_recv.at[z, x], has_up, None)
    spread(z, other, 1, w_recv.at[z, 1 - x], has_up, None)

    for xs in range(2):
        for ys in range(2):
            s = 2 * xs + ys
            view = gall.at[pl.ds(xs * rows, rows), pl.ds(ys * width, width)]
            own = (x == xs) & (y == ys)

            @pl.when(lead & own)
            def _():
                pltpu.make_async_copy(g_ref, view, local_sem.at[2]).wait()

            @pl.when(lead & jnp.logical_not(own))
            def _():
                arrived(view, g_fwd.at[s], g_recv.at[s])

            send(view, view, g_fwd.at[s], g_recv.at[s], sibling, lead)

    for s in range(4):
        @pl.when(jnp.logical_not(lead))
        def _():
            arrived(
                gall.at[pl.ds((s // 2) * rows, rows), pl.ds((s % 2) * width, width)],
                g_fwd.at[s], g_recv.at[s],
            )

    take(doc_part, kp_send.at[2, 0], kp_recv.at[2, 0])

    def take_half(i):
        for n, win in enumerate((kwin, vwin)):
            take(
                win_part(win, half_cols(i, backward_order)), kp_send.at[i, n], kp_recv.at[i, n]
            )

    window = 3 * rows
    here = pl.ds(pl.multiple_of(x * rows, rows), rows)
    there = pl.ds(pl.multiple_of((1 - x) * rows, rows), rows)
    t_pos = lax.broadcasted_iota(jnp.int32, (rows, window), 0) + 2 * rows
    j_pos = lax.broadcasted_iota(jnp.int32, (rows, window), 1)
    doc_col = jnp.transpose(jnp.broadcast_to(doc_ref[...], (DH, rows)))[:, 0:1]
    mask = (doc_col == dwin[0:1, :]) & (j_pos <= t_pos)

    def head_of(i):
        return i + (heads - 1 - 2 * i) * backward_order

    def cols_of(i):
        return pl.ds(pl.multiple_of(head_of(i) * DH, DH), DH)

    def forward(i):
        hc = cols_of(i)
        scores = dot(q_ref[:, hc], kwin[:, hc], ((1,), (1,))) * scale
        scores = jnp.where(mask, scores, NEGATIVE)
        top = jnp.max(scores, axis=1, keepdims=True)
        weights = jnp.where(mask, jnp.exp(scores - top), 0.0)
        inverse = 1.0 / jnp.sum(weights, axis=1, keepdims=True)
        out = dot(weights.astype(BF16), vwin[:, hc], ((1,), (0,))) * inverse
        probs_all[head_of(i)] = weights * inverse
        attn_pair[here, hc] = out.astype(BF16)
        view = attn_pair.at[here, hc]
        send(view, view, at_send.at[i], at_recv.at[i], pair)

    def partial(i):
        arrived(attn_pair.at[there, cols_of(i)], at_send.at[i], at_recv.at[i])
        part[head_of(i)] = dot(attn_pair[:, cols_of(i)], gall[...], ((0,), (0,)))

    def w_round(r):
        for u in range(2):
            view_of = pl.ds(u * unit, unit)

            @pl.when(z - r >= 0)
            def _():
                arrived(wall.at[z - r, view_of, :], w_send.at[0, 2 * r + u], w_recv.at[z - r, u])

            if r < LINE - 1:
                spread(
                    z - r, view_of, 2 * r + u, w_recv.at[z - r, u], (z - r >= 0) & has_up, None
                )

            @pl.when(z + r < LINE)
            def _():
                arrived(wall.at[z + r, view_of, :], w_send.at[1, 2 * r + u], w_recv.at[z + r, u])

            if r < LINE - 1:
                send(
                    wall.at[z + r, view_of, :], wall.at[z + r, view_of, :],
                    w_send.at[1, 2 * r + u], w_recv.at[z + r, u], down, (z + r < LINE) & has_down,
                )

    def sum_step(s):
        b_up = LINE - 1 - s + z
        b_down = s - (LINE - 1) + z
        goes_up = (z <= s) & has_up
        goes_down = (LINE - 1 - z <= s) & has_down

        @pl.when(goes_up & jnp.logical_not(has_down))
        def _():
            up_out[s] = part[b_up].astype(BF16)

        @pl.when(goes_up & has_down)
        def _():
            arrived(up_in.at[b_up], up_send.at[s], up_recv.at[b_up])
            up_out[s] = (part[b_up] + up_in[b_up].astype(F32)).astype(BF16)

        send(up_out.at[s], up_in.at[b_up], up_send.at[s], up_recv.at[b_up], up, goes_up)

        @pl.when(goes_down & jnp.logical_not(has_up))
        def _():
            down_out[s] = part[b_down].astype(BF16)

        @pl.when(goes_down & has_up)
        def _():
            arrived(down_in.at[b_down], down_send.at[s], down_recv.at[b_down])
            down_out[s] = (part[b_down] + down_in[b_down].astype(F32)).astype(BF16)

        send(
            down_out.at[s], down_in.at[b_down], down_send.at[s], down_recv.at[b_down],
            down, goes_down,
        )

    take_half(0)
    forward(0)
    forward(1)
    partial(0)
    sum_step(0)
    take_half(1)
    forward(2)
    w_round(1)
    forward(3)
    partial(1)
    partial(2)
    partial(3)
    w_round(2)
    sum_step(1)
    w_round(3)

    for h in range(heads):
        ga = dot(gall[...], wall[h], ((1,), (1,)))
        ga_own[h] = ga
        ga_out[h] = ga_own[h, there, :].astype(BF16)
        send(ga_out.at[h], ga_in.at[h], ga_send.at[h], ga_recv.at[h], pair)

    sum_step(2)

    def fold(h):
        @pl.when((x == 0) | has_down)
        def _():
            arrived(fold_in.at[h], fold_send.at[h], fold_recv.at[h])

        @pl.when((x == 1) & has_down)
        def _():
            fold_out[h] = (grads_out[h, 1].astype(F32) + fold_in[h].astype(F32)).astype(BF16)

        send(
            fold_out.at[h], grads_in.at[h], gr_send.at[h, 1], gr_recv.at[h],
            down, (x == 1) & has_down,
        )

        @pl.when(x == 0)
        def _():
            own_grads[h] = own_grads[h] + fold_in[h].astype(F32)

    for h in range(heads):
        hc = pl.ds(h * DH, DH)
        arrived(ga_in.at[h], ga_send.at[h], ga_recv.at[h])
        ga = (ga_own[h, here, :] + ga_in[h].astype(F32)).astype(BF16)
        delta = jnp.sum(
            ga.astype(F32) * attn_pair[here, hc].astype(F32), axis=1, keepdims=True
        )
        probs = probs_all[h]
        grad_v = dot(probs.astype(BF16), ga, ((0,), (0,)))
        grad_p = dot(ga, vwin[:, hc], ((1,), (1,)))
        grad_s = (probs * (grad_p - delta)).astype(BF16)
        dq_ref[:, hc] = (dot(grad_s, kwin[:, hc], ((1,), (0,))) * scale).astype(BF16)
        grad_k = dot(grad_s, q_ref[:, hc], ((0,), (0,))) * scale
        grads_out[h, 0, :, pl.ds(0, DH)] = grad_k[rows:2 * rows].astype(BF16)
        grads_out[h, 0, :, pl.ds(DH, DH)] = grad_v[rows:2 * rows].astype(BF16)
        send(
            grads_out.at[h, 0], fold_in.at[h], fold_send.at[h], fold_recv.at[h],
            pair, (x == 1) | has_down,
        )
        grads_out[h, 1, :, pl.ds(0, DH)] = grad_k[0:rows].astype(BF16)
        grads_out[h, 1, :, pl.ds(DH, DH)] = grad_v[0:rows].astype(BF16)
        send(
            grads_out.at[h, 1], grads_in.at[h], gr_send.at[h, 0], gr_recv.at[h],
            down, (x == 0) & has_down,
        )
        own_grads[h, :, pl.ds(0, DH)] = grad_k[2 * rows:]
        own_grads[h, :, pl.ds(DH, DH)] = grad_v[2 * rows:]
        if h > 0:
            fold(h - 1)
    fold(heads - 1)

    @pl.when(has_down)
    def _():
        arrived(up_in.at[z], up_send.at[0], up_recv.at[z])
        part[z] = part[z] + up_in[z].astype(F32)

    @pl.when(has_up)
    def _():
        arrived(down_in.at[z], down_send.at[0], down_recv.at[z])
        part[z] = part[z] + down_in[z].astype(F32)

    pair_out[...] = part[z, other, :].astype(BF16)
    send(pair_out, pair_in, px_send, px_recv, pair)
    for xs in range(2):
        @pl.when(x == xs)
        def _():
            for j in range(2):
                gw_ref[:, pl.ds((2 * j + xs) * width, width)] = part[
                    z, pl.ds(xs * unit, unit), pl.ds(j * width, width)
                ]

    for h in range(heads):
        hc = pl.ds(h * DH, DH)
        @pl.when(has_up)
        def _():
            arrived(grads_in.at[h], gr_send.at[h, 0], gr_recv.at[h])
            own_grads[h] = own_grads[h] + grads_in[h].astype(F32)

        total = own_grads[h]
        dk_ref[:, hc] = total[:, :DH].astype(BF16)
        dv_ref[:, hc] = total[:, DH:].astype(BF16)

    arrived(pair_in, px_send, px_recv)
    for xs in range(2):
        @pl.when(x == xs)
        def _():
            for j in range(2):
                gw_ref[:, pl.ds((2 * j + 1 - xs) * width, width)] = pair_in[
                    :, pl.ds(j * width, width)
                ].astype(F32)

    for cond, finish in pending:
        if cond is None:
            finish()
        else:
            pl.when(cond)(finish)


def handed_on(*refs):
    copies = [pltpu.make_async_copy(refs[i], refs[4 + i], refs[8].at[i]) for i in range(4)]
    for copy in copies:
        copy.start()
    for copy in copies:
        copy.wait()


def shards_pairs(query, key, value, doc_ids, out_weight, grad_out):
    rows, cols = query.shape
    heads = cols // DH
    unit, feats = out_weight.shape
    width = grad_out.shape[1]
    half = 2 * width
    dma = pltpu.SemaphoreType.DMA
    vm = pl.BlockSpec(memory_space=pltpu.VMEM)
    hbm = pl.BlockSpec(memory_space=pl.ANY)
    shapes = (
        jax.ShapeDtypeStruct((rows, cols), BF16),
        jax.ShapeDtypeStruct((rows, cols), BF16),
        jax.ShapeDtypeStruct((rows, cols), BF16),
        jax.ShapeDtypeStruct((unit, feats), F32),
    )
    outs = pl.pallas_call(
        pair_kernel,
        out_shape=shapes,
        in_specs=[vm] * 6,
        out_specs=(vm,) * 4,
        scratch_shapes=[
            pltpu.VMEM((8, rows), jnp.int32),
            pltpu.VMEM((3 * rows, cols), BF16),
            pltpu.VMEM((3 * rows, cols), BF16),
            pltpu.VMEM((8, 3 * rows), jnp.int32),
            pltpu.VMEM((LINE, 2 * unit, half), BF16),
            pltpu.VMEM((2 * rows, half), BF16),
            pltpu.VMEM((2 * rows, cols), BF16),
            pltpu.VMEM((heads, rows, 3 * rows), F32),
            pltpu.VMEM((LINE, 2 * unit, half), F32),
            pltpu.VMEM((LINE - 1, 2 * unit, half), BF16),
            pltpu.VMEM((LINE - 1, 2 * unit, half), BF16),
            pltpu.VMEM((LINE, 2 * unit, half), BF16),
            pltpu.VMEM((LINE, 2 * unit, half), BF16),
            pltpu.VMEM((unit, half), BF16),
            pltpu.VMEM((unit, half), BF16),
            pltpu.VMEM((heads, 2 * rows, DH), F32),
            pltpu.VMEM((heads, rows, DH), BF16),
            pltpu.VMEM((heads, rows, DH), BF16),
            pltpu.VMEM((heads, rows, 2 * DH), F32),
            pltpu.VMEM((heads, 2, rows, 2 * DH), BF16),
            pltpu.VMEM((heads, rows, 2 * DH), BF16),
            pltpu.VMEM((heads, rows, 2 * DH), BF16),
            pltpu.VMEM((heads, rows, 2 * DH), BF16),
            dma((3,)),
            dma((2,)), dma((2,)),
            dma((2, 2 * LINE)), dma((LINE, 2)),
            dma((2,)), dma((4,)), dma((4,)),
            dma((3, 2)), dma((3, 2)),
            dma((3, 2)), dma((3, 2)), dma((3, 2)),
            dma((heads,)), dma((heads,)),
            dma((LINE,)), dma((LINE,)), dma((LINE,)), dma((LINE,)),
            dma, dma,
            dma((heads,)), dma((heads,)),
            dma((heads, 2)), dma((heads,)),
            dma((heads,)), dma((heads,)),
        ],
        compiler_params=pltpu.CompilerParams(
            collective_id=0, has_side_effects=True, vmem_limit_bytes=56 * 1024 * 1024
        ),
    )(query, key, value, doc_ids[None, :], out_weight, grad_out)
    return pl.pallas_call(
        handed_on,
        out_shape=shapes,
        in_specs=[hbm] * 4,
        out_specs=(hbm,) * 4,
        scratch_shapes=[dma((4,))],
    )(*outs)


def solution(mesh):
    return jax.shard_map(
        shards_pairs if mesh.shape["ctx"] == 8 and mesh.shape["fsdp"] == 4 else shards_general,
        mesh=mesh,
        in_specs=(
            P("ctx", "fsdp"),
            P("ctx", "fsdp"),
            P("ctx", "fsdp"),
            P("ctx"),
            P(("fsdp", "ctx"), None),
            P("ctx", "fsdp"),
        ),
        out_specs=(P("ctx", "fsdp"), P("ctx", "fsdp"), P("ctx", "fsdp"), P(("fsdp", "ctx"), None)),
        check_vma=False,
    )
```

```python
import math

import jax
import jax.numpy as jnp
from jax import lax
from jax.experimental import pallas as pl
from jax.experimental.pallas import tpu as pltpu
from jax.sharding import PartitionSpec as P

DH = 128


NEGATIVE = -1e30


def shifted(array, axis, by):
    devices = lax.axis_size(axis)
    pairs = [(i, i + by) for i in range(devices) if 0 <= i + by < devices]
    return lax.ppermute(array, axis, pairs)


def as_sent(array):

    def short(part):
        return part.astype(jnp.bfloat16) if part.dtype == jnp.float32 else part

    return jax.tree.map(short, array)


def passed_along(block, axis, distance):
    devices = range(lax.axis_size(axis))
    route = [((i - distance) % len(devices), i) for i in devices]
    return lax.ppermute(block, axis, route)


def shards_general(query, key, value, doc_ids, out_weight, grad_out):
    tok_rows = query.shape[0]
    feature_width = query.shape[1]
    head_count = feature_width // DH
    cycle_size = lax.axis_size("ctx")
    cycle_reach = max(cycle_size // 8, 2)
    cycle_index = lax.axis_index("ctx")
    score_scale = 1.0 / math.sqrt(DH)
    local_pos = jnp.arange(tok_rows, dtype=jnp.int32)
    own_pos = cycle_index * tok_rows + local_pos
    own_docs = doc_ids + 1
    query_heads = query.reshape(tok_rows, head_count, DH)
    key_heads = key.reshape(tok_rows, head_count, DH)
    value_heads = value.reshape(tok_rows, head_count, DH)

    def scores_of(query_block, key_block):
        return (
            jnp.einsum("tnd,snd->nts", query_block, key_block, preferred_element_type=jnp.float32)
            * score_scale
        )

    state = (
        jnp.full((head_count, tok_rows), NEGATIVE, jnp.float32),
        jnp.zeros((head_count, tok_rows), jnp.float32),
        jnp.zeros((head_count, tok_rows, DH), jnp.float32),
    )
    key_block, value_block = (key_heads, value_heads)
    key_docs = own_docs
    stored_blocks = []
    for cycle_step in range(cycle_reach + 1):
        if cycle_step > 0:
            key_block, value_block = shifted((key_block, value_block), "ctx", 1)
            key_docs = shifted(key_docs, "ctx", 1)
        key_pos = own_pos - cycle_step * tok_rows
        pair_mask = (own_docs[:, None] == key_docs[None, :]) & (
            key_pos[None, :] <= own_pos[:, None]
        )
        forward_row_max, forward_row_sum, forward_output_sum = state
        forward_scores = jnp.where(pair_mask[None], scores_of(query_heads, key_block), NEGATIVE)
        new_max = jnp.maximum(forward_row_max, jnp.max(forward_scores, axis=-1))
        decay_factor = jnp.exp(forward_row_max - new_max)
        forward_weights = jnp.where(
            pair_mask[None], jnp.exp(forward_scores - new_max[..., None]), 0.0
        )
        new_sum = forward_row_sum * decay_factor + jnp.sum(forward_weights, axis=-1)
        weights_low = forward_weights.astype(jnp.bfloat16)
        new_output = forward_output_sum * decay_factor[..., None] + jnp.einsum(
            "nts,snd->ntd", weights_low, value_block, preferred_element_type=jnp.float32
        )
        state = (new_max, new_sum, new_output)
        stored_blocks.append((key_block, value_block, pair_mask))
    row_max, row_sum, output_sum = state
    log_total = row_max + jnp.log(row_sum)
    attn_heads = (output_sum / row_sum[..., None]).astype(jnp.bfloat16).transpose(1, 0, 2)
    attention = attn_heads.reshape(tok_rows, feature_width)
    grad_full = lax.all_gather(grad_out, "fsdp", axis=1, tiled=True)
    grad_attn = lax.dot_general(
        grad_full,
        lax.all_gather(out_weight, "ctx", axis=0, tiled=True),
        (((1,), (1,)), ((), ())),
        preferred_element_type=jnp.float32,
    ).astype(jnp.bfloat16)
    grad_weight = lax.psum_scatter(
        lax.dot_general(
            attention, grad_full, (((0,), (0,)), ((), ())), preferred_element_type=jnp.float32
        ),
        "ctx",
        scatter_dimension=0,
        tiled=True,
    )
    grad_heads = grad_attn.reshape(tok_rows, head_count, DH)
    delta_sum = jnp.einsum(
        "tnd,tnd->nt", grad_heads, attn_heads, preferred_element_type=jnp.float32
    )
    grad_query = jnp.zeros((tok_rows, head_count, DH), jnp.float32)
    carried = None
    for cycle_step in range(cycle_reach + 1):
        key_block, value_block, pair_mask = stored_blocks[cycle_step]
        if cycle_step > 0:
            carried = jax.tree.map(
                lambda part, own: part.astype(own.dtype),
                passed_along(as_sent(carried), "ctx", 1),
                carried,
            )
        scores = scores_of(query_heads, key_block)
        weights = jnp.where(pair_mask[None], jnp.exp(scores - log_total[..., None]), 0.0)
        rounded = weights.astype(jnp.bfloat16)
        value_part = jnp.einsum(
            "nts,tnd->snd", rounded, grad_heads, preferred_element_type=jnp.float32
        )
        grad_weights = jnp.einsum(
            "tnd,snd->nts", grad_heads, value_block, preferred_element_type=jnp.float32
        )
        grad_scores = (weights * (grad_weights - delta_sum[..., None])).astype(jnp.bfloat16)
        query_part = (
            jnp.einsum("nts,snd->tnd", grad_scores, key_block, preferred_element_type=jnp.float32)
            * score_scale
        )
        key_part = (
            jnp.einsum("nts,tnd->snd", grad_scores, query_heads, preferred_element_type=jnp.float32)
            * score_scale
        )
        query_part, key_part, value_part = (query_part, key_part, value_part)
        grad_query = grad_query + query_part
        if cycle_step == 0:
            carried = (key_part, value_part)
        else:
            carried = (carried[0] + key_part, carried[1] + value_part)
    grad_key, grad_value = jax.tree.map(
        lambda part, own: part.astype(own.dtype),
        passed_along(as_sent(carried), "ctx", -cycle_reach),
        carried,
    )
    return (
        grad_query.reshape(tok_rows, feature_width).astype(jnp.bfloat16),
        grad_key.reshape(tok_rows, feature_width).astype(jnp.bfloat16),
        grad_value.reshape(tok_rows, feature_width).astype(jnp.bfloat16),
        grad_weight,
    )


LINE = 4
F32 = jnp.float32
BF16 = jnp.bfloat16


def dot(a, b, dims):
    return lax.dot_general(a, b, (dims, ((), ())), preferred_element_type=F32)


def pair_kernel(
    q_ref, k_ref, v_ref, doc_ref, w_ref, g_ref,
    dq_ref, dk_ref, dv_ref, gw_ref,
    docs, kwin, vwin, dwin, wall, gall, attn_pair, probs_all, part, up_out, down_out, up_in, down_in,
    pair_out, pair_in, ga_own, ga_out, ga_in, own_grads, grads_out, grads_in,
    fold_in, fold_out,
    local_sem, wx_send, wx_recv, w_send, w_recv, g_send, g_fwd, g_recv, kv_send, kv_recv,
    kp_send, kp_fwd, kp_recv,
    at_send, at_recv, up_send, up_recv, down_send, down_recv, px_send, px_recv,
    ga_send, ga_recv, gr_send, gr_recv, fold_send, fold_recv,
):
    c = lax.axis_index("ctx")
    f = lax.axis_index("fsdp")
    z, x = c // 2, c % 2
    y, core = f // 2, f % 2
    rows = q_ref.shape[0]
    heads = q_ref.shape[1] // DH
    unit = w_ref.shape[0]
    width = g_ref.shape[1]
    scale = 1.0 / math.sqrt(DH)
    pending = []

    def remote(src, dst, ss, rs, dev):
        return pltpu.make_async_remote_copy(
            src_ref=src, dst_ref=dst, send_sem=ss, recv_sem=rs,
            device_id=dev, device_id_type=pl.DeviceIdType.MESH,
        )

    def send(src, dst, ss, rs, dev, cond=None):
        def start():
            remote(src, dst, ss, rs, dev).start()

        def finish():
            remote(src, dst, ss, rs, dev).wait_send()

        if cond is None:
            start()
        else:
            pl.when(cond)(start)
        pending.append((cond, finish))

    def arrived(dst, ss, rs):
        remote(dst, dst, ss, rs, (c, f)).wait_recv()

    pair = (c + 1 - 2 * x, f)
    up = (c + 2, f)
    down = (c - 2, f)
    has_up, has_down = z < LINE - 1, z > 0

    barrier = pltpu.get_barrier_semaphore()

    def greet(dev):
        pl.semaphore_signal(barrier, inc=1, device_id=dev, device_id_type=pl.DeviceIdType.MESH)

    greet(pair)
    greet((c, f + 1 - 2 * core))
    greet((c, f + 2 - 4 * y))
    greet((c + 1 - 2 * x, f + 2 - 4 * y))
    pl.when(has_up)(lambda: greet(up))
    pl.when(has_down)(lambda: greet(down))
    pl.semaphore_wait(barrier, 4 + (z + LINE - 1) // LINE + (2 * LINE - 2 - z) // LINE)

    docs[...] = jnp.broadcast_to(doc_ref[...], (8, rows))
    halfc = heads * DH // 2
    backward_order = 1 - z // 2
    backward_order_up = 1 - (z + 1) // 2
    first, second, last = (pl.ds(i * rows, rows) for i in range(3))

    def half_cols(i, backward):
        return pl.ds(pl.multiple_of((i + (1 - 2 * i) * backward) * halfc, halfc), halfc)

    send(docs, dwin.at[:, first], kv_send.at[2, 0], kv_recv.at[2, 0], up, has_up)
    send(docs, dwin.at[:, second], kp_send.at[2, 0], kp_recv.at[2, 0], pair, x == 0)
    for i in range(2):
        hu, hp = half_cols(i, backward_order_up), half_cols(i, backward_order)
        for n, (own, win) in enumerate(((k_ref, kwin), (v_ref, vwin))):
            send(own.at[:, hu], win.at[first, hu], kv_send.at[i, n], kv_recv.at[i, n], up, has_up)
            send(own.at[:, hp], win.at[second, hp], kp_send.at[i, n], kp_recv.at[i, n], pair, x == 0)

    mine = pl.ds(pl.multiple_of(x * unit, unit), unit)
    other = pl.ds(pl.multiple_of((1 - x) * unit, unit), unit)
    for j in range(2):
        cols = pl.ds(pl.multiple_of(2 * j * width + (1 - x) * width, width), width)
        send(
            w_ref.at[:, cols], wall.at[z, mine, pl.ds(j * width, width)],
            wx_send.at[j], wx_recv.at[j], pair,
        )
    local = []
    for j in range(2):
        cols = pl.ds(pl.multiple_of(2 * j * width + x * width, width), width)
        copy = pltpu.make_async_copy(
            w_ref.at[:, cols], wall.at[z, mine, pl.ds(j * width, width)], local_sem.at[j]
        )
        copy.start()
        local.append(copy)

    block = gall.at[
        pl.ds(pl.multiple_of(x * rows, rows), rows), pl.ds(pl.multiple_of(y * width, width), width)
    ]
    lead = core == x
    taker = 2 * z + core
    send(
        g_ref, block, g_send.at[0], g_recv.at[2 * x + y], (taker, 2 * (1 - y) + core)
    )
    send(
        g_ref, block, g_send.at[1], g_recv.at[2 * x + y], (taker, 2 * y + core), core != x
    )
    sibling = (c, f + 1 - 2 * core)

    @pl.when(lead)
    def _():
        pltpu.make_async_copy(g_ref, block, local_sem.at[2]).start()

    for copy in local:
        copy.wait()

    def spread(zb, rows_of, slot, rs, upward, downward):
        view = wall.at[zb, rows_of, :]
        if upward is not None:
            send(view, view, w_send.at[0, slot], rs, up, upward)
        if downward is not None:
            send(view, view, w_send.at[1, slot], rs, down, downward)

    spread(z, mine, 0, w_recv.at[z, x], None, has_down)
    for j in range(2):
        arrived(wall.at[z, other, pl.ds(j * width, width)], wx_send.at[j], wx_recv.at[j])
    spread(z, other, 1, w_recv.at[z, 1 - x], None, has_down)

    kwin[last, :] = k_ref[...]
    vwin[last, :] = v_ref[...]
    dwin[:, last] = docs[...]

    def nothing(slot):
        kwin[slot, :] = jnp.zeros((rows, heads * DH), BF16)
        vwin[slot, :] = jnp.zeros((rows, heads * DH), BF16)
        dwin[:, slot] = jnp.full((8, rows), -1, jnp.int32)

    pl.when(z == 0)(lambda: nothing(first))
    pl.when((z == 0) & (x == 0))(lambda: nothing(second))

    relay = (x == 1) & has_down

    def relayed(part_of, ss, rs, fs, ps):
        src = part_of(first)

        @pl.when(has_down)
        def _():
            arrived(src, ss, rs)

        send(src, part_of(second), fs, ps, pair, relay)

    def take(part_of, ss, ps):
        @pl.when((x == 1) | has_down)
        def _():
            arrived(part_of(second), ss, ps)

    def win_part(win, cols):
        return lambda slot: win.at[slot, cols]

    def doc_part(slot):
        return dwin.at[:, slot]

    relayed(doc_part, kv_send.at[2, 0], kv_recv.at[2, 0], kp_fwd.at[2, 0], kp_recv.at[2, 0])
    for i in range(2):
        for n, win in enumerate((kwin, vwin)):
            relayed(
                win_part(win, half_cols(i, backward_order)),
                kv_send.at[i, n], kv_recv.at[i, n], kp_fwd.at[i, n], kp_recv.at[i, n],
            )
    spread(z, mine, 0, w_recv.at[z, x], has_up, None)
    spread(z, other, 1, w_recv.at[z, 1 - x], has_up, None)

    for xs in range(2):
        for ys in range(2):
            s = 2 * xs + ys
            view = gall.at[pl.ds(xs * rows, rows), pl.ds(ys * width, width)]
            own = (x == xs) & (y == ys)

            @pl.when(lead & own)
            def _():
                pltpu.make_async_copy(g_ref, view, local_sem.at[2]).wait()

            @pl.when(lead & jnp.logical_not(own))
            def _():
                arrived(view, g_fwd.at[s], g_recv.at[s])

            send(view, view, g_fwd.at[s], g_recv.at[s], sibling, lead)

    for s in range(4):
        @pl.when(jnp.logical_not(lead))
        def _():
            arrived(
                gall.at[pl.ds((s // 2) * rows, rows), pl.ds((s % 2) * width, width)],
                g_fwd.at[s], g_recv.at[s],
            )

    take(doc_part, kp_send.at[2, 0], kp_recv.at[2, 0])

    def take_half(i):
        for n, win in enumerate((kwin, vwin)):
            take(
                win_part(win, half_cols(i, backward_order)), kp_send.at[i, n], kp_recv.at[i, n]
            )

    window = 3 * rows
    here = pl.ds(pl.multiple_of(x * rows, rows), rows)
    there = pl.ds(pl.multiple_of((1 - x) * rows, rows), rows)
    t_pos = lax.broadcasted_iota(jnp.int32, (rows, window), 0) + 2 * rows
    j_pos = lax.broadcasted_iota(jnp.int32, (rows, window), 1)
    doc_col = jnp.transpose(jnp.broadcast_to(doc_ref[...], (DH, rows)))[:, 0:1]
    mask = (doc_col == dwin[0:1, :]) & (j_pos <= t_pos)

    def head_of(i):
        return i + (heads - 1 - 2 * i) * backward_order

    def cols_of(i):
        return pl.ds(pl.multiple_of(head_of(i) * DH, DH), DH)

    def forward(i):
        hc = cols_of(i)
        scores = dot(q_ref[:, hc], kwin[:, hc], ((1,), (1,))) * scale
        scores = jnp.where(mask, scores, NEGATIVE)
        top = jnp.max(scores, axis=1, keepdims=True)
        weights = jnp.where(mask, jnp.exp(scores - top), 0.0)
        inverse = 1.0 / jnp.sum(weights, axis=1, keepdims=True)
        out = dot(weights.astype(BF16), vwin[:, hc], ((1,), (0,))) * inverse
        probs_all[head_of(i)] = weights * inverse
        attn_pair[here, hc] = out.astype(BF16)
        view = attn_pair.at[here, hc]
        send(view, view, at_send.at[i], at_recv.at[i], pair)

    def partial(i):
        arrived(attn_pair.at[there, cols_of(i)], at_send.at[i], at_recv.at[i])
        part[head_of(i)] = dot(attn_pair[:, cols_of(i)], gall[...], ((0,), (0,)))

    def w_round(r):
        for u in range(2):
            view_of = pl.ds(u * unit, unit)

            @pl.when(z - r >= 0)
            def _():
                arrived(wall.at[z - r, view_of, :], w_send.at[0, 2 * r + u], w_recv.at[z - r, u])

            if r < LINE - 1:
                spread(
                    z - r, view_of, 2 * r + u, w_recv.at[z - r, u], (z - r >= 0) & has_up, None
                )

            @pl.when(z + r < LINE)
            def _():
                arrived(wall.at[z + r, view_of, :], w_send.at[1, 2 * r + u], w_recv.at[z + r, u])

            if r < LINE - 1:
                send(
                    wall.at[z + r, view_of, :], wall.at[z + r, view_of, :],
                    w_send.at[1, 2 * r + u], w_recv.at[z + r, u], down, (z + r < LINE) & has_down,
                )

    def sum_step(s):
        b_up = LINE - 1 - s + z
        b_down = s - (LINE - 1) + z
        goes_up = (z <= s) & has_up
        goes_down = (LINE - 1 - z <= s) & has_down

        @pl.when(goes_up & jnp.logical_not(has_down))
        def _():
            up_out[s] = part[b_up].astype(BF16)

        @pl.when(goes_up & has_down)
        def _():
            arrived(up_in.at[b_up], up_send.at[s], up_recv.at[b_up])
            up_out[s] = (part[b_up] + up_in[b_up].astype(F32)).astype(BF16)

        send(up_out.at[s], up_in.at[b_up], up_send.at[s], up_recv.at[b_up], up, goes_up)

        @pl.when(goes_down & jnp.logical_not(has_up))
        def _():
            down_out[s] = part[b_down].astype(BF16)

        @pl.when(goes_down & has_up)
        def _():
            arrived(down_in.at[b_down], down_send.at[s], down_recv.at[b_down])
            down_out[s] = (part[b_down] + down_in[b_down].astype(F32)).astype(BF16)

        send(
            down_out.at[s], down_in.at[b_down], down_send.at[s], down_recv.at[b_down],
            down, goes_down,
        )

    take_half(0)
    forward(0)
    forward(1)
    partial(0)
    sum_step(0)
    take_half(1)
    forward(2)
    w_round(1)
    forward(3)
    partial(1)
    partial(2)
    partial(3)
    w_round(2)
    sum_step(1)
    w_round(3)

    for h in range(heads):
        ga = dot(gall[...], wall[h], ((1,), (1,)))
        ga_own[h] = ga
        ga_out[h] = ga_own[h, there, :].astype(BF16)
        send(ga_out.at[h], ga_in.at[h], ga_send.at[h], ga_recv.at[h], pair)

    sum_step(2)

    def fold(h):
        @pl.when((x == 0) | has_down)
        def _():
            arrived(fold_in.at[h], fold_send.at[h], fold_recv.at[h])

        @pl.when((x == 1) & has_down)
        def _():
            fold_out[h] = (grads_out[h, 1].astype(F32) + fold_in[h].astype(F32)).astype(BF16)

        send(
            fold_out.at[h], grads_in.at[h], gr_send.at[h, 1], gr_recv.at[h],
            down, (x == 1) & has_down,
        )

        @pl.when(x == 0)
        def _():
            own_grads[h] = own_grads[h] + fold_in[h].astype(F32)

    for h in range(heads):
        hc = pl.ds(h * DH, DH)
        arrived(ga_in.at[h], ga_send.at[h], ga_recv.at[h])
        ga = (ga_own[h, here, :] + ga_in[h].astype(F32)).astype(BF16)
        delta = jnp.sum(
            ga.astype(F32) * attn_pair[here, hc].astype(F32), axis=1, keepdims=True
        )
        probs = probs_all[h]
        grad_v = dot(probs.astype(BF16), ga, ((0,), (0,)))
        grad_p = dot(ga, vwin[:, hc], ((1,), (1,)))
        grad_s = (probs * (grad_p - delta)).astype(BF16)
        dq_ref[:, hc] = (dot(grad_s, kwin[:, hc], ((1,), (0,))) * scale).astype(BF16)
        grad_k = dot(grad_s, q_ref[:, hc], ((0,), (0,))) * scale
        grads_out[h, 0, :, pl.ds(0, DH)] = grad_k[rows:2 * rows].astype(BF16)
        grads_out[h, 0, :, pl.ds(DH, DH)] = grad_v[rows:2 * rows].astype(BF16)
        send(
            grads_out.at[h, 0], fold_in.at[h], fold_send.at[h], fold_recv.at[h],
            pair, (x == 1) | has_down,
        )
        grads_out[h, 1, :, pl.ds(0, DH)] = grad_k[0:rows].astype(BF16)
        grads_out[h, 1, :, pl.ds(DH, DH)] = grad_v[0:rows].astype(BF16)
        send(
            grads_out.at[h, 1], grads_in.at[h], gr_send.at[h, 0], gr_recv.at[h],
            down, (x == 0) & has_down,
        )
        own_grads[h, :, pl.ds(0, DH)] = grad_k[2 * rows:]
        own_grads[h, :, pl.ds(DH, DH)] = grad_v[2 * rows:]
        if h > 0:
            fold(h - 1)
    fold(heads - 1)

    @pl.when(has_down)
    def _():
        arrived(up_in.at[z], up_send.at[0], up_recv.at[z])
        part[z] = part[z] + up_in[z].astype(F32)

    @pl.when(has_up)
    def _():
        arrived(down_in.at[z], down_send.at[0], down_recv.at[z])
        part[z] = part[z] + down_in[z].astype(F32)

    pair_out[...] = part[z, other, :].astype(BF16)
    send(pair_out, pair_in, px_send, px_recv, pair)
    for xs in range(2):
        @pl.when(x == xs)
        def _():
            for j in range(2):
                gw_ref[:, pl.ds((2 * j + xs) * width, width)] = part[
                    z, pl.ds(xs * unit, unit), pl.ds(j * width, width)
                ]

    for h in range(heads):
        hc = pl.ds(h * DH, DH)
        @pl.when(has_up)
        def _():
            arrived(grads_in.at[h], gr_send.at[h, 0], gr_recv.at[h])
            own_grads[h] = own_grads[h] + grads_in[h].astype(F32)

        total = own_grads[h]
        dk_ref[:, hc] = total[:, :DH].astype(BF16)
        dv_ref[:, hc] = total[:, DH:].astype(BF16)

    arrived(pair_in, px_send, px_recv)
    for xs in range(2):
        @pl.when(x == xs)
        def _():
            for j in range(2):
                gw_ref[:, pl.ds((2 * j + 1 - xs) * width, width)] = pair_in[
                    :, pl.ds(j * width, width)
                ].astype(F32)

    for cond, finish in pending:
        if cond is None:
            finish()
        else:
            pl.when(cond)(finish)


def handed_on(*refs):
    held, sems = refs[8:12], refs[12]
    inward = [pltpu.make_async_copy(refs[i], held[i], sems.at[0, i]) for i in range(4)]
    outward = [pltpu.make_async_copy(held[i], refs[4 + i], sems.at[1, i]) for i in range(4)]
    for copy in inward:
        copy.start()
    for i in range(4):
        inward[i].wait()
        outward[i].start()
    for copy in outward:
        copy.wait()


def shards_pairs(query, key, value, doc_ids, out_weight, grad_out):
    rows, cols = query.shape
    heads = cols // DH
    unit, feats = out_weight.shape
    width = grad_out.shape[1]
    half = 2 * width
    dma = pltpu.SemaphoreType.DMA
    vm = pl.BlockSpec(memory_space=pltpu.VMEM)
    hbm = pl.BlockSpec(memory_space=pl.ANY)
    shapes = (
        jax.ShapeDtypeStruct((rows, cols), BF16),
        jax.ShapeDtypeStruct((rows, cols), BF16),
        jax.ShapeDtypeStruct((rows, cols), BF16),
        jax.ShapeDtypeStruct((unit, feats), F32),
    )
    outs = pl.pallas_call(
        pair_kernel,
        out_shape=shapes,
        in_specs=[vm] * 6,
        out_specs=(vm,) * 4,
        scratch_shapes=[
            pltpu.VMEM((8, rows), jnp.int32),
            pltpu.VMEM((3 * rows, cols), BF16),
            pltpu.VMEM((3 * rows, cols), BF16),
            pltpu.VMEM((8, 3 * rows), jnp.int32),
            pltpu.VMEM((LINE, 2 * unit, half), BF16),
            pltpu.VMEM((2 * rows, half), BF16),
            pltpu.VMEM((2 * rows, cols), BF16),
            pltpu.VMEM((heads, rows, 3 * rows), F32),
            pltpu.VMEM((LINE, 2 * unit, half), F32),
            pltpu.VMEM((LINE - 1, 2 * unit, half), BF16),
            pltpu.VMEM((LINE - 1, 2 * unit, half), BF16),
            pltpu.VMEM((LINE, 2 * unit, half), BF16),
            pltpu.VMEM((LINE, 2 * unit, half), BF16),
            pltpu.VMEM((unit, half), BF16),
            pltpu.VMEM((unit, half), BF16),
            pltpu.VMEM((heads, 2 * rows, DH), F32),
            pltpu.VMEM((heads, rows, DH), BF16),
            pltpu.VMEM((heads, rows, DH), BF16),
            pltpu.VMEM((heads, rows, 2 * DH), F32),
            pltpu.VMEM((heads, 2, rows, 2 * DH), BF16),
            pltpu.VMEM((heads, rows, 2 * DH), BF16),
            pltpu.VMEM((heads, rows, 2 * DH), BF16),
            pltpu.VMEM((heads, rows, 2 * DH), BF16),
            dma((3,)),
            dma((2,)), dma((2,)),
            dma((2, 2 * LINE)), dma((LINE, 2)),
            dma((2,)), dma((4,)), dma((4,)),
            dma((3, 2)), dma((3, 2)),
            dma((3, 2)), dma((3, 2)), dma((3, 2)),
            dma((heads,)), dma((heads,)),
            dma((LINE,)), dma((LINE,)), dma((LINE,)), dma((LINE,)),
            dma, dma,
            dma((heads,)), dma((heads,)),
            dma((heads, 2)), dma((heads,)),
            dma((heads,)), dma((heads,)),
        ],
        compiler_params=pltpu.CompilerParams(
            collective_id=0, has_side_effects=True, vmem_limit_bytes=56 * 1024 * 1024
        ),
    )(query, key, value, doc_ids[None, :], out_weight, grad_out)
    return pl.pallas_call(
        handed_on,
        out_shape=shapes,
        in_specs=[hbm] * 4,
        out_specs=(hbm,) * 4,
        scratch_shapes=[pltpu.VMEM(shape.shape, shape.dtype) for shape in shapes] + [dma((2, 4))],
    )(*outs)


def solution(mesh):
    return jax.shard_map(
        shards_pairs if mesh.shape["ctx"] == 8 and mesh.shape["fsdp"] == 4 else shards_general,
        mesh=mesh,
        in_specs=(
            P("ctx", "fsdp"),
            P("ctx", "fsdp"),
            P("ctx", "fsdp"),
            P("ctx"),
            P(("fsdp", "ctx"), None),
            P("ctx", "fsdp"),
        ),
        out_specs=(P("ctx", "fsdp"), P("ctx", "fsdp"), P("ctx", "fsdp"), P(("fsdp", "ctx"), None)),
        check_vma=False,
    )
```
